32 devices in a mesh: section: 2 (over x), tok: 16 (over z, y, core).
Axes of the slice: x: 2, y: 2, z: 4, core: 2. Of those that a mesh axis runs over, the one named last changes fastest.
Arguments:
- queries: bfloat16 [2, 4096, 4096], P('section', 'tok'), may hold values from -120 to 120
- suffix_kv: bfloat16 [2, 4096, 1024], P('section', 'tok'), may hold values from -4 to 4
- prefix_kv: bfloat16 [2, 16, 64, 1024], P('section', 'tok'), may hold values from -4 to 4
- served: int32 [2, 32, 8], P('section'), may hold values from -1 to 15, as said below
Outputs:
- passed: bfloat16 [2, 4096, 4096], P('section', 'tok')
The draws below stay inside these ranges and needn't reach their ends.
Inputs may be any that keep to these rules, and one draw needn't show every extreme that they name: `served`: entry k of a row is -1 or a page in [k * 2, (k + 1) * 2); live entries come first, then -1; entry 0 is always live, and block 0 of every section has all 8 live.
All inputs are finite; a program needn't handle non-finite values.
Results may differ from the reference program's by a relative error of at most 0.0029.
Values may be sent and summed in bfloat16 or wider, within the bound.
A program may use at most 64 MiB of HBM per device.

```python
import math
import jax
import jax.numpy as jnp
from jax import lax

Q_HEADS = 32
KV_HEADS = 4
HEAD = 128
BLOCK = 128
PAGE = 64
DEPTH = 8
PB = 16
WIDE = 2
QB = 32
N_SECTION = 2


def joint_draw(key):
    base_key = jax.random.fold_in(key, 11)
    key_query, key_pairs = jax.random.split(base_key)
    pair_shape = (N_SECTION, QB, BLOCK, 2 * KV_HEADS * HEAD)
    query_shape = (N_SECTION, QB, BLOCK, Q_HEADS * HEAD)
    pairs = jnp.clip(jax.random.normal(key_pairs, pair_shape, jnp.float32), -4.0, 4.0)
    query_vals = jnp.clip(2.5 * jax.random.normal(key_query, query_shape, jnp.float32), -10.0, 10.0)
    query_vals = query_vals.reshape(N_SECTION, QB * BLOCK, Q_HEADS * HEAD)
    pairs = pairs.reshape(N_SECTION, QB * BLOCK, 2 * KV_HEADS * HEAD)
    return (query_vals, pairs)


def draw_queries(key, part):
    return joint_draw(key)[0].astype(jnp.bfloat16)


def draw_suffix_kv(key, part):
    return joint_draw(key)[1].astype(jnp.bfloat16)


def draw_served(key, part):
    key_pick, key_count = jax.random.split(jax.random.fold_in(key, 5))
    offsets = (jnp.arange(DEPTH) * WIDE).astype(jnp.int32)
    picks = jax.random.randint(key_pick, (N_SECTION, QB, DEPTH), 0, WIDE).astype(jnp.int32) + offsets
    counts = jax.random.randint(key_count, (N_SECTION, QB, 1), 1, DEPTH + 1).astype(jnp.int32)
    counts = counts.at[:, 0, :].set(DEPTH)
    slot_pos = lax.broadcasted_iota(jnp.int32, (N_SECTION, QB, DEPTH), 2)
    return jnp.where(slot_pos < counts, picks, -1).astype(jnp.int32)


def level_of(key, extent, shards, least, top_value):
    def one(axis_at, blocks):
        steps = jax.random.uniform(jax.random.fold_in(jax.random.fold_in(key, 6), axis_at), (blocks,), jnp.float32, least / len(shards), top_value / len(shards))
        return jnp.repeat(jnp.exp(steps), extent[axis_at] // blocks).reshape((-1,) + (1,) * (len(extent) - axis_at - 1))

    level = one(*shards[0])
    for cut in shards[1:]:
        level = level * one(*cut)
    return level


def noise(stream_key, shape, spread, most, cuts=(), dtype=jnp.bfloat16):
    level = level_of(stream_key, shape, cuts, -0.22, 0.18) if cuts else 1.0
    entries = jax.random.normal(stream_key, shape, jnp.float32) * spread * level
    return jnp.minimum(jnp.maximum(entries, -most), most).astype(dtype)


def setup_inputs(seed: int = 0) -> dict:
    splits = jax.random.split(jax.random.key(seed), 5)
    queries = draw_queries(jax.random.fold_in(splits[4], 71), 0)
    suffix_kv = draw_suffix_kv(jax.random.fold_in(splits[4], 71), 0)
    prefix_kv = noise(splits[2], (N_SECTION, PB, PAGE, 2 * KV_HEADS * HEAD), 1.0, 4.0, ((0, 2), (1, 16)))
    served = draw_served(jax.random.fold_in(splits[4], 71), 0)
    return dict(queries=queries, suffix_kv=suffix_kv, prefix_kv=prefix_kv, served=served)


def attend(query_rows, key_rows, value_rows, allowed, score_scale):
    scores = jnp.einsum('qgd,kd->gqk', query_rows.astype(jnp.float32), key_rows.astype(jnp.float32)) * score_scale
    scores = jnp.where(allowed[None], scores, -jnp.inf)
    row_top = lax.optimization_barrier(jnp.max(scores, axis=2, keepdims=True))
    exponent = jnp.exp(scores - row_top)
    totals = lax.optimization_barrier(jnp.sum(exponent, axis=2))
    weights = lax.optimization_barrier(exponent.astype(jnp.bfloat16)).astype(jnp.float32)
    mixture = jnp.einsum('gqk,kd->qgd', weights, value_rows.astype(jnp.float32))
    return (mixture / jnp.transpose(totals)[:, :, None]).astype(jnp.bfloat16)

def reference(queries, suffix_kv, prefix_kv, served):
    sections = queries.shape[0]
    group_size = Q_HEADS // KV_HEADS
    score_scale = 1.0 / math.sqrt(HEAD)
    query_blocks = queries.reshape(sections, QB, BLOCK, KV_HEADS, group_size, HEAD)
    own_pairs = suffix_kv.reshape(sections, QB, BLOCK, 2, KV_HEADS, HEAD)
    row_index = lax.broadcasted_iota(jnp.int32, (BLOCK, BLOCK), 0)
    col_index = lax.broadcasted_iota(jnp.int32, (BLOCK, BLOCK), 1)
    causal = col_index <= row_index

    def per_block(position):
        section_id = position // QB
        block_id = position % QB
        picks = served[section_id, block_id]
        prefix_pairs = prefix_kv[section_id][jnp.maximum(picks, 0)]
        prefix_pairs = prefix_pairs.reshape(DEPTH * PAGE, 2, KV_HEADS, HEAD)
        both_pairs = jnp.concatenate([prefix_pairs, own_pairs[section_id, block_id]], axis=0)
        live_rows = jnp.repeat(picks >= 0, PAGE)
        allowed = jnp.concatenate([jnp.broadcast_to(live_rows[None], (BLOCK, DEPTH * PAGE)), causal], axis=1)

        def per_head(query_rows, key_rows, value_rows):
            return attend(query_rows, key_rows, value_rows, allowed, score_scale)
        head_outputs = jax.vmap(per_head, in_axes=(1, 1, 1), out_axes=1)(query_blocks[section_id, block_id], both_pairs[:, 0], both_pairs[:, 1])
        return head_outputs.reshape(BLOCK, Q_HEADS * HEAD)
    blocks_out = lax.map(per_block, jnp.arange(sections * QB))
    attention = blocks_out.reshape(sections, QB * BLOCK, Q_HEADS * HEAD)
    return jnp.roll(attention, 1, axis=0)
```

```python
import functools
import math

import jax
import jax.numpy as jnp
from jax import lax
from jax.experimental import pallas as pl
from jax.experimental.pallas import tpu as pltpu
from jax.sharding import PartitionSpec as P

HEAD = 128
BLOCK = 128
CORES = 2
MESH = pl.DeviceIdType.MESH
NEG = float("-inf")


def kernel(dims, served, q_hbm, suf_hbm, pre_hbm, out_hbm, *scratch):
    sections, far, near, kv_heads, depth, page, per_dev, group, unit = dims
    pages = scratch[:kv_heads]
    (q_v, suf_v, stage, keys, vals, q_sem, suf_sem, page_sem, s1, r1, s2, r2, s3, r3, s_out, r_out) = scratch[kv_heads:]
    tok = lax.axis_index("tok")
    sec = lax.axis_index("section")
    c = lax.rem(tok, CORES)
    b = lax.rem(tok // CORES, near)
    a = tok // (CORES * near)
    own = depth * page
    width = unit * HEAD
    units = group // unit

    def at(x, y, z):
        return {"tok": (x * near + y) * CORES + z}

    loads = []
    for h in range(kv_heads):
        for part in range(2):
            col = (part * kv_heads + h) * HEAD
            loads.append(
                pltpu.make_async_copy(
                    pre_hbm.at[0, 0, :, pl.ds(col, HEAD)], pages[h].at[c, b, a, part], page_sem.at[h, part]
                )
            )
    for load in loads:
        load.start()
    suf_load = pltpu.make_async_copy(suf_hbm.at[0], suf_v, suf_sem)
    suf_load.start()

    barrier = pltpu.get_barrier_semaphore()
    partners = [at(lax.rem(a + d, far), b, c) for d in range(1, far)]
    partners += [at(a, lax.rem(b + d, near), c) for d in range(1, near)]
    partners += [at(a, b, 1 - c)]
    ahead = {"section": lax.rem(sec + 1, sections)}
    partners += [ahead]
    if sections > 2:
        partners += [{"section": lax.rem(sec + sections - 1, sections)}]
    for partner in partners:
        pl.semaphore_signal(barrier, inc=1, device_id=partner, device_id_type=MESH)

    q_loads = {}
    for h in range(kv_heads):
        for blk in range(per_dev):
            where = (pl.ds(blk * BLOCK, BLOCK), pl.ds(h * group * HEAD, group * HEAD))
            q_loads[h, blk] = pltpu.make_async_copy(
                q_hbm.at[(0,) + where], q_v.at[where], q_sem.at[h, blk]
            )
            q_loads[h, blk].start()
    pl.semaphore_wait(barrier, len(partners))

    def remote(ref_src, ref_dst, send, recv, target):
        return pltpu.make_async_remote_copy(
            src_ref=ref_src, dst_ref=ref_dst, send_sem=send, recv_sem=recv, device_id=target, device_id_type=MESH
        )

    def first(h):
        return [
            remote(
                pages[h].at[c, b, a], pages[h].at[c, b, a], s1.at[h, d - 1], r1.at[h, d - 1],
                at(lax.rem(a + d, far), b, c),
            )
            for d in range(1, far)
        ]

    def second(h):
        return [
            remote(
                pages[h].at[c, b], pages[h].at[c, b], s2.at[h, d - 1], r2.at[h, d - 1],
                at(a, lax.rem(b + d, near), c),
            )
            for d in range(1, near)
        ]

    def third(h):
        return [remote(pages[h].at[c], pages[h].at[c], s3.at[h], r3.at[h], at(a, b, 1 - c))]

    def go(copies):
        for copy in copies:
            copy.start()

    def arrive(copies):
        for copy in copies:
            copy.wait_recv()

    def gone(copies):
        for copy in copies:
            copy.wait_send()

    def own_page(h):
        loads[2 * h].wait()
        loads[2 * h + 1].wait()

    def send_out(h, blk, u):
        where = (pl.ds(blk * BLOCK, BLOCK), pl.ds(pl.multiple_of((h * units + u) * width, width), width))
        index = (h * per_dev + blk) * units + u
        return remote(stage.at[where], out_hbm.at[(0,) + where], s_out.at[index], r_out.at[index], ahead)

    factor = math.log2(math.e) / math.sqrt(HEAD)
    causal = lax.broadcasted_iota(jnp.int32, (BLOCK, BLOCK), 1) <= lax.broadcasted_iota(
        jnp.int32, (BLOCK, BLOCK), 0
    )
    causal_bias = jnp.where(causal, 0.0, NEG).astype(jnp.float32)
    column = lax.broadcasted_iota(jnp.int32, (1, own), 1)

    def attend(h, blk):
        row = tok * per_dev + blk
        live = jnp.int32(0)
        for k in range(depth):
            pick = served[0, row, k]
            live = live + jnp.where(pick >= 0, 1, 0).astype(jnp.int32)
            pick = jnp.maximum(pick, 0)
            pc = lax.rem(pick, CORES)
            pb = lax.rem(lax.div(pick, CORES), near)
            pa = lax.div(pick, CORES * near)
            keys[pl.ds(k * page, page), :] = pages[h][pc, pb, pa, 0]
            vals[pl.ds(k * page, page), :] = pages[h][pc, pb, pa, 1]
        rows = pl.ds(blk * BLOCK, BLOCK)
        keys[pl.ds(own, BLOCK), :] = suf_v[rows, pl.ds(h * HEAD, HEAD)]
        vals[pl.ds(own, BLOCK), :] = suf_v[rows, pl.ds((kv_heads + h) * HEAD, HEAD)]
        bias = jnp.where(column < live * page, 0.0, NEG).astype(jnp.float32)
        q_loads[h, blk].wait()

        def step(u, carry):
            for j in range(unit):
                cols = pl.ds(pl.multiple_of(((h * units + u) * unit + j) * HEAD, HEAD), HEAD)
                scores = lax.dot_general(
                    q_v[rows, cols], keys[...], (((1,), (1,)), ((), ())), preferred_element_type=jnp.float32
                )
                left = scores[:, :own] + bias
                right = scores[:, own:] + causal_bias
                top = jnp.maximum(
                    jnp.max(left, axis=1, keepdims=True), jnp.max(right, axis=1, keepdims=True)
                )
                left = jnp.exp2((left - top) * factor)
                right = jnp.exp2((right - top) * factor)
                total = jnp.sum(left, axis=1, keepdims=True) + jnp.sum(right, axis=1, keepdims=True)
                weights = jnp.concatenate([left.astype(jnp.bfloat16), right.astype(jnp.bfloat16)], axis=1)
                mixed = jnp.dot(weights, vals[...], preferred_element_type=jnp.float32)
                stage[rows, cols] = (mixed / total).astype(jnp.bfloat16)
            send_out(h, blk, u).start()
            return carry

        lax.fori_loop(0, units, step, 0)

    p1 = [first(h) for h in range(kv_heads)]
    p2 = [second(h) for h in range(kv_heads)]
    p3 = [third(h) for h in range(kv_heads)]
    own_page(0)
    go(p1[0])
    arrive(p1[0])
    go(p2[0])
    own_page(1)
    go(p1[1])
    arrive(p2[0])
    go(p3[0])
    suf_load.wait()
    arrive(p3[0])
    for h in range(kv_heads):
        if h + 1 < kv_heads:
            arrive(p1[h + 1])
            go(p2[h + 1])
        if h + 2 < kv_heads:
            own_page(h + 2)
            go(p1[h + 2])
        for blk in range(per_dev):
            attend(h, blk)
            if blk == 0 and h + 1 < kv_heads:
                arrive(p2[h + 1])
                go(p3[h + 1])
        if h + 1 < kv_heads:
            arrive(p3[h + 1])
    for h in range(kv_heads):
        gone(p1[h])
        gone(p2[h])
        gone(p3[h])
    for h in range(kv_heads):
        for blk in range(per_dev):

            def finish(u, carry):
                copy = send_out(h, blk, u)
                copy.wait_send()
                copy.wait_recv()
                return carry

            lax.fori_loop(0, units, finish, 0)


def on_device(sections, toks, queries, suffix_kv, prefix_kv, served):
    rows, q_width = queries.shape[1:]
    kv_width = suffix_kv.shape[2]
    kv_heads = kv_width // (2 * HEAD)
    group = q_width // HEAD // kv_heads
    page = prefix_kv.shape[2]
    depth = served.shape[2]
    per_dev = rows // BLOCK
    chips = toks // CORES
    near = 1
    while 4 * near * near <= chips:
        near *= 2
    far = chips // near
    unit = 2
    dims = (sections, far, near, kv_heads, depth, page, per_dev, group, unit)
    keys = depth * page + BLOCK
    sends = kv_heads * group // unit * per_dev
    dma = pltpu.SemaphoreType.DMA
    any_ = pl.BlockSpec(memory_space=pl.ANY)
    bf16 = jnp.bfloat16
    return pl.pallas_call(
        functools.partial(kernel, dims),
        out_shape=jax.ShapeDtypeStruct(queries.shape, bf16),
        in_specs=[pl.BlockSpec(memory_space=pltpu.SMEM), any_, any_, any_],
        out_specs=any_,
        scratch_shapes=[pltpu.VMEM((CORES, near, far, 2, page, HEAD), bf16) for _ in range(kv_heads)]
        + [
            pltpu.VMEM((rows, q_width), bf16),
            pltpu.VMEM((rows, kv_width), bf16),
            pltpu.VMEM((rows, q_width), bf16),
            pltpu.VMEM((keys, HEAD), bf16),
            pltpu.VMEM((keys, HEAD), bf16),
            dma((kv_heads, per_dev)),
            dma,
            dma((kv_heads, 2)),
            dma((kv_heads, max(far - 1, 1))),
            dma((kv_heads, max(far - 1, 1))),
            dma((kv_heads, max(near - 1, 1))),
            dma((kv_heads, max(near - 1, 1))),
            dma((kv_heads,)),
            dma((kv_heads,)),
            dma((sends,)),
            dma((sends,)),
        ],
        compiler_params=pltpu.CompilerParams(
            collective_id=0, has_side_effects=True, vmem_limit_bytes=48 * 1024 * 1024
        ),
    )(served, queries, suffix_kv, prefix_kv)


def solution(mesh):
    placed = (
        P("section", "tok", None),
        P("section", "tok", None),
        P("section", "tok", None, None),
        P("section", None, None),
    )
    run = functools.partial(on_device, mesh.shape["section"], mesh.shape["tok"])
    return jax.shard_map(
        run, mesh=mesh, in_specs=placed, out_specs=P("section", "tok", None), check_vma=False
    )
```

```python
import functools
import math

import jax
import jax.numpy as jnp
from jax import lax
from jax.experimental import pallas as pl
from jax.experimental.pallas import tpu as pltpu
from jax.sharding import PartitionSpec as P

HEAD = 128
BLOCK = 128
CORES = 2
MESH = pl.DeviceIdType.MESH
NEG = float("-inf")


def kernel(dims, served_hbm, q_hbm, suf_hbm, pre_hbm, out_hbm, *scratch):
    sections, far, near, kv_heads, depth, page, per_dev, group, unit = dims
    pages = scratch[:kv_heads]
    (served, served_sem, q_v, suf_v, stage, keys, vals, q_sem, suf_sem, page_sem, s1, r1, s2, r2, s3, r3, s_out, r_out) = scratch[kv_heads:]
    tok = lax.axis_index("tok")
    sec = lax.axis_index("section")
    c = lax.rem(tok, CORES)
    b = lax.rem(tok // CORES, near)
    a = tok // (CORES * near)
    own = depth * page
    width = unit * HEAD
    units = group // unit

    def at(x, y, z):
        return {"tok": (x * near + y) * CORES + z}

    served_load = pltpu.make_async_copy(served_hbm, served, served_sem)
    served_load.start()
    loads = []
    for h in range(kv_heads):
        for part in range(2):
            col = (part * kv_heads + h) * HEAD
            loads.append(
                pltpu.make_async_copy(
                    pre_hbm.at[0, 0, :, pl.ds(col, HEAD)], pages[h].at[c, b, a, part], page_sem.at[h, part]
                )
            )
    for load in loads:
        load.start()
    suf_load = pltpu.make_async_copy(suf_hbm.at[0], suf_v, suf_sem)
    suf_load.start()

    barrier = pltpu.get_barrier_semaphore()
    partners = [at(lax.rem(a + d, far), b, c) for d in range(1, far)]
    partners += [at(a, lax.rem(b + d, near), c) for d in range(1, near)]
    partners += [at(a, b, 1 - c)]
    ahead = {"section": lax.rem(sec + 1, sections)}
    partners += [ahead]
    if sections > 2:
        partners += [{"section": lax.rem(sec + sections - 1, sections)}]
    for partner in partners:
        pl.semaphore_signal(barrier, inc=1, device_id=partner, device_id_type=MESH)

    q_loads = {}
    for h in range(kv_heads):
        for blk in range(per_dev):
            where = (pl.ds(blk * BLOCK, BLOCK), pl.ds(h * group * HEAD, group * HEAD))
            q_loads[h, blk] = pltpu.make_async_copy(
                q_hbm.at[(0,) + where], q_v.at[where], q_sem.at[h, blk]
            )
            q_loads[h, blk].start()
    pl.semaphore_wait(barrier, len(partners))

    def remote(ref_src, ref_dst, send, recv, target):
        return pltpu.make_async_remote_copy(
            src_ref=ref_src, dst_ref=ref_dst, send_sem=send, recv_sem=recv, device_id=target, device_id_type=MESH
        )

    def first(h):
        return [
            remote(
                pages[h].at[c, b, a], pages[h].at[c, b, a], s1.at[h, d - 1], r1.at[h, d - 1],
                at(lax.rem(a + d, far), b, c),
            )
            for d in range(1, far)
        ]

    def second(h):
        return [
            remote(
                pages[h].at[c, b], pages[h].at[c, b], s2.at[h, d - 1], r2.at[h, d - 1],
                at(a, lax.rem(b + d, near), c),
            )
            for d in range(1, near)
        ]

    def third(h):
        return [remote(pages[h].at[c], pages[h].at[c], s3.at[h], r3.at[h], at(a, b, 1 - c))]

    def go(copies):
        for copy in copies:
            copy.start()

    def arrive(copies):
        for copy in copies:
            copy.wait_recv()

    def gone(copies):
        for copy in copies:
            copy.wait_send()

    def own_page(h):
        loads[2 * h].wait()
        loads[2 * h + 1].wait()

    def send_out(h, blk, u):
        where = (pl.ds(blk * BLOCK, BLOCK), pl.ds(pl.multiple_of((h * units + u) * width, width), width))
        index = (h * per_dev + blk) * units + u
        return remote(stage.at[where], out_hbm.at[(0,) + where], s_out.at[index], r_out.at[index], ahead)

    factor = math.log2(math.e) / math.sqrt(HEAD)
    causal = lax.broadcasted_iota(jnp.int32, (BLOCK, BLOCK), 1) <= lax.broadcasted_iota(
        jnp.int32, (BLOCK, BLOCK), 0
    )
    causal_bias = jnp.where(causal, 0.0, NEG).astype(jnp.float32)
    column = lax.broadcasted_iota(jnp.int32, (1, own), 1)

    def attend(h, blk):
        row = tok * per_dev + blk
        live = jnp.int32(0)
        for k in range(depth):
            pick = served[0, row, k]
            live = live + jnp.where(pick >= 0, 1, 0).astype(jnp.int32)
            pick = jnp.maximum(pick, 0)
            pc = lax.rem(pick, CORES)
            pb = lax.rem(lax.div(pick, CORES), near)
            pa = lax.div(pick, CORES * near)
            keys[pl.ds(k * page, page), :] = pages[h][pc, pb, pa, 0]
            vals[pl.ds(k * page, page), :] = pages[h][pc, pb, pa, 1]
        rows = pl.ds(blk * BLOCK, BLOCK)
        keys[pl.ds(own, BLOCK), :] = suf_v[rows, pl.ds(h * HEAD, HEAD)]
        vals[pl.ds(own, BLOCK), :] = suf_v[rows, pl.ds((kv_heads + h) * HEAD, HEAD)]
        bias = jnp.where(column < live * page, 0.0, NEG).astype(jnp.float32)
        q_loads[h, blk].wait()

        def step(u, carry):
            for j in range(unit):
                cols = pl.ds(pl.multiple_of(((h * units + u) * unit + j) * HEAD, HEAD), HEAD)
                scores = lax.dot_general(
                    q_v[rows, cols], keys[...], (((1,), (1,)), ((), ())), preferred_element_type=jnp.float32
                )
                left = scores[:, :own] + bias
                right = scores[:, own:] + causal_bias
                top = jnp.maximum(
                    jnp.max(left, axis=1, keepdims=True), jnp.max(right, axis=1, keepdims=True)
                )
                left = jnp.exp2((left - top) * factor)
                right = jnp.exp2((right - top) * factor)
                total = jnp.sum(left, axis=1, keepdims=True) + jnp.sum(right, axis=1, keepdims=True)
                weights = jnp.concatenate([left.astype(jnp.bfloat16), right.astype(jnp.bfloat16)], axis=1)
                mixed = jnp.dot(weights, vals[...], preferred_element_type=jnp.float32)
                stage[rows, cols] = (mixed / total).astype(jnp.bfloat16)
            send_out(h, blk, u).start()
            return carry

        lax.fori_loop(0, units, step, 0)

    p1 = [first(h) for h in range(kv_heads)]
    p2 = [second(h) for h in range(kv_heads)]
    p3 = [third(h) for h in range(kv_heads)]
    own_page(0)
    go(p1[0])
    arrive(p1[0])
    go(p2[0])
    own_page(1)
    go(p1[1])
    arrive(p2[0])
    go(p3[0])
    suf_load.wait()
    served_load.wait()
    arrive(p3[0])
    for h in range(kv_heads):
        if h + 1 < kv_heads:
            arrive(p1[h + 1])
            go(p2[h + 1])
        if h + 2 < kv_heads:
            own_page(h + 2)
            go(p1[h + 2])
        for blk in range(per_dev):
            attend(h, blk)
            if blk == 0 and h + 1 < kv_heads:
                arrive(p2[h + 1])
                go(p3[h + 1])
        if h + 1 < kv_heads:
            arrive(p3[h + 1])
    for h in range(kv_heads):
        gone(p1[h])
        gone(p2[h])
        gone(p3[h])
    for h in range(kv_heads):
        for blk in range(per_dev):

            def finish(u, carry):
                copy = send_out(h, blk, u)
                copy.wait_send()
                copy.wait_recv()
                return carry

            lax.fori_loop(0, units, finish, 0)


def on_device(sections, toks, queries, suffix_kv, prefix_kv, served):
    rows, q_width = queries.shape[1:]
    kv_width = suffix_kv.shape[2]
    kv_heads = kv_width // (2 * HEAD)
    group = q_width // HEAD // kv_heads
    page = prefix_kv.shape[2]
    depth = served.shape[2]
    per_dev = rows // BLOCK
    chips = toks // CORES
    near = 1
    while 4 * near * near <= chips:
        near *= 2
    far = chips // near
    unit = 2
    dims = (sections, far, near, kv_heads, depth, page, per_dev, group, unit)
    keys = depth * page + BLOCK
    sends = kv_heads * group // unit * per_dev
    dma = pltpu.SemaphoreType.DMA
    any_ = pl.BlockSpec(memory_space=pl.ANY)
    bf16 = jnp.bfloat16
    return pl.pallas_call(
        functools.partial(kernel, dims),
        out_shape=jax.ShapeDtypeStruct(queries.shape, bf16),
        in_specs=[pl.BlockSpec(memory_space=pltpu.HBM)] * 4,
        out_specs=any_,
        scratch_shapes=[pltpu.VMEM((CORES, near, far, 2, page, HEAD), bf16) for _ in range(kv_heads)]
        + [
            pltpu.SMEM(served.shape, served.dtype),
            dma,
            pltpu.VMEM((rows, q_width), bf16),
            pltpu.VMEM((rows, kv_width), bf16),
            pltpu.VMEM((rows, q_width), bf16),
            pltpu.VMEM((keys, HEAD), bf16),
            pltpu.VMEM((keys, HEAD), bf16),
            dma((kv_heads, per_dev)),
            dma,
            dma((kv_heads, 2)),
            dma((kv_heads, max(far - 1, 1))),
            dma((kv_heads, max(far - 1, 1))),
            dma((kv_heads, max(near - 1, 1))),
            dma((kv_heads, max(near - 1, 1))),
            dma((kv_heads,)),
            dma((kv_heads,)),
            dma((sends,)),
            dma((sends,)),
        ],
        compiler_params=pltpu.CompilerParams(
            collective_id=0, has_side_effects=True, vmem_limit_bytes=61 * 1024 * 1024
        ),
    )(served, queries, suffix_kv, prefix_kv)


def solution(mesh):
    placed = (
        P("section", "tok", None),
        P("section", "tok", None),
        P("section", "tok", None, None),
        P("section", None, None),
    )
    run = functools.partial(on_device, mesh.shape["section"], mesh.shape["tok"])
    return jax.shard_map(
        run, mesh=mesh, in_specs=placed, out_specs=P("section", "tok", None), check_vma=False
    )
```
